128 devices in a mesh: dp: 16 (over y, z_hi, core), tensor: 8 (over z_lo, x).
Axes of the slice: x: 4, y: 4, z: 4 (z_hi: 2, z_lo: 2; z = z_hi * 2 + z_lo), core: 2. Of those that a mesh axis runs over, the one named last changes fastest.
Arguments:
- inputs: bfloat16 [8192, 6144], P(('dp', 'tensor')), may hold values from -24 to 24
- upstream: bfloat16 [8192, 6144], P(('dp', 'tensor')), may hold values from -6 to 6
- w_qkv: bfloat16 [3, 6144, 3072], P(None, None, 'tensor'), may hold values from -0.078125 to 0.078125
- w_out: bfloat16 [3072, 6144], P('tensor'), may hold values from -0.109375 to 0.109375
- ln_gain: float32 [6144], replicated, may hold values from 0.25 to 1.75
Outputs:
- grad_inputs: bfloat16 [8192, 6144], P(('dp', 'tensor'))
- grad_qkv: float32 [3, 6144, 3072], P(None, 'dp', 'tensor')
- grad_out: float32 [3072, 6144], P('tensor', 'dp')
- grad_gain: float32 [6144], replicated
The draws below stay inside these ranges and needn't reach their ends.
All inputs are finite; a program needn't handle non-finite values.
Results may differ from the reference program's by a relative error of at most 0.019.
Values may be sent and summed in bfloat16 or wider, within the bound.
No kernel may reach another device: no remote copies, remote signals or barrier semaphores. Data moves between devices by JAX's collectives and lax.ppermute only.
A program may use at most 192 MiB of HBM per device.

```python
import math
import jax
import jax.numpy as jnp
from jax import lax

D = 6144
HEADS = 24
HD = 128
LEN = 512
TOKENS = 8192
HC = 3072
N_DP = 16
N_TENSOR = 8


def with_spikes(values, key, source, target, parts, factor):
    def block_of(dim):
        return (jnp.arange(values.shape[dim]) // (values.shape[dim] // parts)).reshape((-1,) + (1,) * (values.ndim - 1 - dim))

    one_side = jax.random.permutation(key, parts)[block_of(target)]
    second = (block_of(target) + parts // 2) % parts
    return jnp.where((block_of(source) == one_side) | (block_of(source) == second), factor * values, values)


def steps_of(rng, extent, pieces, smallest, largest):
    loudness = 1.0
    for axis_at, parts in pieces:
        heights = jax.random.uniform(jax.random.fold_in(jax.random.fold_in(rng, 6), axis_at), (parts,), jnp.float32, smallest / len(pieces), largest / len(pieces))
        loudness = loudness * jnp.repeat(jnp.exp(heights), extent[axis_at] // parts).reshape((-1,) + (1,) * (len(extent) - 1 - axis_at))
    return loudness


def normal_values(own_key, shape, width, most, cuts=(), held_as=jnp.bfloat16):
    values = width * jax.random.normal(own_key, shape, jnp.float32)
    if cuts:
        values = values * steps_of(own_key, shape, cuts, -0.22, 0.18)
    return jnp.clip(values, -most, most).astype(held_as)


def heavy_noise(own_key, extent, deviation, bound, cuts, heavy, kind=jnp.bfloat16):
    entries = deviation * jax.random.normal(own_key, extent, jnp.float32)
    if cuts:
        entries = entries * steps_of(own_key, extent, cuts, -0.22, 0.18)
    return jnp.clip(with_spikes(entries, jax.random.fold_in(own_key, 3), *heavy), -bound, bound).astype(kind)


def setup_inputs(seed: int = 0) -> dict:
    arg_keys = jax.random.split(jax.random.key(seed), 6)
    return {
        "inputs": heavy_noise(arg_keys[0], (TOKENS, D), 1.0, 24.0, ((0, 128),), (0, 1, 128, 5.5)),
        "upstream": normal_values(arg_keys[1], (TOKENS, D), 1.0, 6.0, ((0, 128),)),
        "w_qkv": normal_values(arg_keys[2], (3, D, HC), D ** -0.5, 0.078125, ((2, 8),)),
        "w_out": normal_values(arg_keys[3], (HC, D), HC ** -0.5, 0.109375, ((0, 8),)),
        "ln_gain": jnp.clip(1.0 + 0.15 * jax.random.normal(arg_keys[4], (D,), jnp.float32), 0.25, 1.75),
    }


EPSILON = 1e-06

def layer_stats(values):
    average = lax.optimization_barrier(jnp.mean(values, axis=-1, keepdims=True))
    centered = values - average
    inverse = lax.rsqrt(lax.optimization_barrier(jnp.mean(centered * centered, axis=-1, keepdims=True)) + EPSILON)
    return (centered * inverse, inverse)

def norm_back(grad, normal, inverse):
    return inverse * (grad - lax.optimization_barrier(jnp.mean(grad, axis=-1, keepdims=True)) - normal * lax.optimization_barrier(jnp.mean(grad * normal, axis=-1, keepdims=True)))

def rounded(values):
    return lax.optimization_barrier(values.astype(jnp.bfloat16)).astype(jnp.float32)

def reference(inputs, upstream, w_qkv, w_out, ln_gain):
    score_scale = 1.0 / math.sqrt(HD)
    all_width = HEADS * HD
    group_count = N_TENSOR
    qkv_full = w_qkv.astype(jnp.float32)
    out_full = w_out.astype(jnp.float32)

    def one_row(sums_so_far, row_pair):
        sum_qkv, sum_out, sum_gain = sums_so_far
        input_row, upstream_row = row_pair
        normal_rows, inverse = layer_stats(input_row.astype(jnp.float32))
        normed = rounded(normal_rows * ln_gain)
        projected = jnp.einsum('td,sdc->tsc', normed, qkv_full).reshape(LEN, 3, HEADS, HD)
        query_hat, query_inv = layer_stats(projected[:, 0])
        key_hat, key_inv = layer_stats(projected[:, 1])
        query_low = rounded(query_hat)
        key_low = rounded(key_hat)
        value_low = rounded(projected[:, 2])
        scores = jnp.einsum('qhd,khd->hqk', query_low, key_low) * score_scale
        exponent = jnp.exp(scores)
        attention = exponent / lax.optimization_barrier(jnp.sum(exponent, axis=-1, keepdims=True))
        attention_low = rounded(attention)
        attended = rounded(jnp.einsum('hqk,khd->qhd', attention_low, value_low)).reshape(LEN, all_width)
        upstream_full = upstream_row.astype(jnp.float32)
        d_attended = rounded(jnp.einsum('td,cd->tc', upstream_full, out_full)).reshape(LEN, HEADS, HD)
        row_out = rounded(jnp.einsum('tc,td->cd', attended, upstream_full))
        d_scores_raw = jnp.einsum('qhd,khd->hqk', d_attended, value_low)
        d_value = rounded(jnp.einsum('hqk,qhd->khd', attention_low, d_attended))
        d_scores = rounded(attention * (d_scores_raw - lax.optimization_barrier(jnp.sum(d_scores_raw * attention, axis=-1, keepdims=True))) * score_scale)
        d_query_low = jnp.einsum('hqk,khd->qhd', d_scores, key_low)
        d_key_low = jnp.einsum('hqk,qhd->khd', d_scores, query_low)
        d_query = rounded(norm_back(d_query_low, query_hat, query_inv))
        d_key = rounded(norm_back(d_key_low, key_hat, key_inv))
        d_projected = jnp.stack([d_query, d_key, d_value], axis=1).reshape(LEN, 3, all_width)
        row_qkv = rounded(jnp.einsum('td,tsc->sdc', normed, d_projected))
        group_terms = jnp.einsum('tsgc,sdgc->gtd', d_projected.reshape(LEN, 3, group_count, all_width // group_count), qkv_full.reshape(3, D, group_count, all_width // group_count))
        d_normed = lax.optimization_barrier(jnp.sum(rounded(group_terms), axis=0))
        row_gain = lax.optimization_barrier(jnp.sum(d_normed * normal_rows, axis=0))
        d_input = (upstream_full + norm_back(d_normed * ln_gain, normal_rows, inverse)).astype(jnp.bfloat16)
        return ((sum_qkv + row_qkv, sum_out + row_out, sum_gain + row_gain), d_input)
    start_sums = (jnp.zeros((3, D, all_width), jnp.float32), jnp.zeros((all_width, D), jnp.float32), jnp.zeros((D,), jnp.float32))
    row_inputs = (inputs.reshape(N_DP, LEN, D), upstream.reshape(N_DP, LEN, D))
    final_sums, grad_rows = lax.scan(one_row, start_sums, row_inputs)
    grad_qkv, grad_out, grad_gain = final_sums
    return (grad_rows.reshape(TOKENS, D), grad_qkv, grad_out, grad_gain)
```

```python
import math

import jax
import jax.numpy as jnp
from jax import lax
from jax.experimental import pallas as pl
from jax.experimental.pallas import tpu as pltpu
from jax.sharding import PartitionSpec as P

HD = 128
EPSILON = 1e-06
D = 6144
W = 384
BF = jnp.bfloat16
F32 = jnp.float32
MIB = 1 << 20

X_FWD = ("tensor", [(z * 4 + x, z * 4 + (x + 1) % 4) for z in range(2) for x in range(4)])
X_BWD = ("tensor", [(z * 4 + x, z * 4 + (x + 3) % 4) for z in range(2) for x in range(4)])
Z_LOW = ("tensor", [(z * 4 + x, (1 - z) * 4 + x) for z in range(2) for x in range(4)])
Y_FWD = ("dp", [(y * 4 + r, (y + 1) % 4 * 4 + r) for y in range(4) for r in range(4)])
Y_BWD = ("dp", [(y * 4 + r, (y + 3) % 4 * 4 + r) for y in range(4) for r in range(4)])
Z_HIGH = ("dp", [(i, i ^ 2) for i in range(16)])
CORE = ("dp", [(i, i ^ 1) for i in range(16)])
BUTTERFLY = [
    CORE,
    ("dp", [(i, i ^ 4) for i in range(16)]),
    Z_HIGH,
    ("tensor", [(i, i ^ 1) for i in range(8)]),
    Z_LOW,
    ("dp", [(i, i ^ 8) for i in range(16)]),
    ("tensor", [(i, i ^ 2) for i in range(8)]),
]


def move(value, route):
    return lax.ppermute(value, route[0], route[1])


def params(limit):
    return pltpu.CompilerParams(vmem_limit_bytes=limit * MIB)


def cost(flops, nbytes):
    return pl.CostEstimate(flops=int(flops), bytes_accessed=int(nbytes), transcendentals=0)


def layer_stats(values):
    average = jnp.mean(values, axis=-1, keepdims=True)
    centered = values - average
    inverse = lax.rsqrt(jnp.mean(centered * centered, axis=-1, keepdims=True) + EPSILON)
    return (centered * inverse, inverse)


def norm_back(grad, normal, inverse):
    return inverse * (
        grad
        - jnp.mean(grad, axis=-1, keepdims=True)
        - normal * jnp.mean(grad * normal, axis=-1, keepdims=True)
    )


def gather_eight(own, fwd, bwd, swap):
    behind = move(own, fwd)
    ahead = move(own, bwd)
    across = move(own, swap)
    from_behind = move(jnp.stack([behind[0], across[0]]), fwd)
    from_ahead = move(jnp.stack([ahead[1], across[1]]), bwd)
    from_across = move(jnp.stack([behind[1], ahead[0]]), swap)
    last_top = move(from_behind[1], fwd)
    last_bottom = move(from_ahead[1], bwd)
    near = (own, behind, ahead, across)
    far = (from_behind, from_ahead, from_across, last_top, last_bottom)
    return near, far


def near_rows(refs):
    return [r[i] for r in refs for i in range(2)]


def far_rows(refs):
    fb, fa, fz, lt, lb = refs
    return [fb[0], fa[0], fb[1], fz[0], fz[1], fa[1], lt[...], lb[...]]


def add(a, b):
    return (a.astype(F32) + b.astype(F32)).astype(BF)


def scatter_eight(terms, fwd, bwd, swap):
    own, behind, ahead, across, opposite, a_behind, a_ahead, a_opposite = terms
    one = move(a_opposite[0], bwd)
    two = move(a_opposite[1], fwd)
    by_swap = move(jnp.stack([a_behind[1], a_ahead[0]]), swap)
    by_bwd = move(jnp.stack([opposite[0], add(a_behind[0], one)]), bwd)
    by_fwd = move(jnp.stack([opposite[1], add(a_ahead[1], two)]), fwd)
    last_bwd = move(add(behind, jnp.stack([by_bwd[0], by_swap[0]])), bwd)
    last_fwd = move(add(ahead, jnp.stack([by_swap[1], by_fwd[0]])), fwd)
    last_swap = move(add(across, jnp.stack([by_bwd[1], by_fwd[1]])), swap)
    return own, last_bwd, last_fwd, last_swap


def norm_rows(pieces, gain, picker):
    def kernel(*refs):
        gain_ref, out_ref = refs[-2], refs[-1]
        for at, rows in enumerate(picker(refs[:-2])):
            normal, _ = layer_stats(rows.astype(F32))
            out_ref[32 * at : 32 * at + 32, :] = (normal * gain_ref[...]).astype(BF)

    return pl.pallas_call(
        kernel,
        out_shape=jax.ShapeDtypeStruct((256, D), BF),
        compiler_params=params(40),
        cost_estimate=cost(256 * D * 10, 256 * D * 4),
        name="norm_rows",
    )(*pieces, gain.reshape(1, D))


def project(normed, weight):
    step = 768

    def kernel(x_ref, w_ref, out_ref):
        @pl.when(pl.program_id(0) == 0)
        def _():
            out_ref[...] = jnp.zeros_like(out_ref)

        for s in range(3):
            out_ref[s] += jnp.dot(x_ref[...], w_ref[s], preferred_element_type=F32)

    return pl.pallas_call(
        kernel,
        grid=(D // step,),
        in_specs=[
            pl.BlockSpec((256, step), lambda k: (0, k)),
            pl.BlockSpec((3, step, W), lambda k: (0, k, 0)),
        ],
        out_specs=pl.BlockSpec((3, 256, W), lambda k: (0, 0, 0)),
        out_shape=jax.ShapeDtypeStruct((3, 256, W), F32),
        compiler_params=params(32),
        cost_estimate=cost(2 * 256 * D * 3 * W, 3 * D * W * 2 + 256 * D * 2),
        name="project",
    )(normed, weight)


def upstream_rows(pieces, w_out, picker):
    step = 768

    def kernel(*refs):
        w_ref, cat_ref, out_ref, acc = refs[-4:]
        k = pl.program_id(0)

        @pl.when(k == 0)
        def _():
            acc[...] = jnp.zeros_like(acc)

        for at, rows in enumerate(picker(refs[:-4])):
            cat_ref[32 * at : 32 * at + 32, :] = rows
        acc[...] += lax.dot_general(
            cat_ref[...], w_ref[...], (((1,), (1,)), ((), ())), preferred_element_type=F32
        )

        @pl.when(k == D // step - 1)
        def _():
            out_ref[...] = acc[...].astype(BF)

    specs = [
        pl.BlockSpec((2, 32, step), lambda k: (0, 0, k))
        if p.ndim == 3
        else pl.BlockSpec((32, step), lambda k: (0, k))
        for p in pieces
    ]
    return pl.pallas_call(
        kernel,
        grid=(D // step,),
        in_specs=specs + [pl.BlockSpec((W, step), lambda k: (0, k))],
        out_specs=[
            pl.BlockSpec((256, step), lambda k: (0, k)),
            pl.BlockSpec((256, W), lambda k: (0, 0)),
        ],
        out_shape=[jax.ShapeDtypeStruct((256, D), BF), jax.ShapeDtypeStruct((256, W), BF)],
        scratch_shapes=[pltpu.VMEM((256, W), F32)],
        compiler_params=params(32),
        cost_estimate=cost(2 * 256 * D * W, D * W * 2 + 256 * D * 4),
        name="upstream_rows",
    )(*pieces, w_out)


def pick_blocks(values, blocks):
    def kernel(_, in_ref, out_ref):
        out_ref[...] = in_ref[...]

    return pl.pallas_call(
        kernel,
        grid_spec=pltpu.PrefetchScalarGridSpec(
            num_scalar_prefetch=1,
            grid=(8,),
            in_specs=[pl.BlockSpec((256, W), lambda k, b: (0, b[k]))],
            out_specs=pl.BlockSpec((256, W), lambda k, b: (0, k)),
        ),
        out_shape=jax.ShapeDtypeStruct((256, 8 * W), BF),
        compiler_params=params(16),
        cost_estimate=cost(0, 256 * 8 * W * 4),
        name="pick_blocks",
    )(blocks, values)


SCALE = 1.0 / math.sqrt(HD)


def dot_nt(a, b):
    return lax.dot_general(a, b, (((1,), (1,)), ((), ())), preferred_element_type=F32)


def dot_tn(a, b):
    return lax.dot_general(a, b, (((0,), (0,)), ((), ())), preferred_element_type=F32)


def dot_nn(a, b):
    return jnp.dot(a, b, preferred_element_type=F32)


def join(one_ref, two_ref, s):
    return jnp.concatenate([one_ref[s], two_ref[s]], axis=0)


def attend_forward(near, far):
    def kernel(one_ref, two_ref, out_ref):
        query, _ = layer_stats(join(one_ref, two_ref, 0))
        key, _ = layer_stats(join(one_ref, two_ref, 1))
        value = join(one_ref, two_ref, 2).astype(BF)
        exponent = jnp.exp(dot_nt(query.astype(BF), key.astype(BF)) * SCALE)
        attention = exponent / jnp.sum(exponent, axis=-1, keepdims=True)
        out_ref[...] = dot_nn(attention.astype(BF), value).astype(BF)

    return pl.pallas_call(
        kernel,
        grid=(W // HD,),
        in_specs=[pl.BlockSpec((3, 256, HD), lambda h: (0, 0, h))] * 2,
        out_specs=pl.BlockSpec((512, HD), lambda h: (0, h)),
        out_shape=jax.ShapeDtypeStruct((512, W), BF),
        compiler_params=params(40),
        cost_estimate=cost(3 * 4 * 512 * 512 * HD, 3 * 512 * W * 4),
        name="attend_forward",
    )(near, far)


def attend_backward(near, far, d_near, d_far):
    def kernel(one_ref, two_ref, d_one, d_two, out_ref):
        query, query_inv = layer_stats(join(one_ref, two_ref, 0))
        key, key_inv = layer_stats(join(one_ref, two_ref, 1))
        value_low = join(one_ref, two_ref, 2).astype(BF)
        query_low = query.astype(BF)
        key_low = key.astype(BF)
        d_att = jnp.concatenate([d_one[...], d_two[...]], axis=0)
        exponent = jnp.exp(dot_nt(query_low, key_low) * SCALE)
        attention = exponent / jnp.sum(exponent, axis=-1, keepdims=True)
        d_raw = dot_nt(d_att, value_low)
        out_ref[2] = dot_tn(attention.astype(BF), d_att).astype(BF)
        inner = jnp.sum(d_raw * attention, axis=-1, keepdims=True)
        d_scores = (attention * (d_raw - inner) * SCALE).astype(BF)
        out_ref[0] = norm_back(dot_nn(d_scores, key_low), query, query_inv).astype(BF)
        out_ref[1] = norm_back(dot_tn(d_scores, query_low), key, key_inv).astype(BF)

    return pl.pallas_call(
        kernel,
        grid=(W // HD,),
        in_specs=[pl.BlockSpec((3, 256, HD), lambda h: (0, 0, h))] * 2
        + [pl.BlockSpec((256, HD), lambda h: (0, h))] * 2,
        out_specs=pl.BlockSpec((3, 512, HD), lambda h: (0, 0, h)),
        out_shape=jax.ShapeDtypeStruct((3, 512, W), BF),
        compiler_params=params(48),
        cost_estimate=cost(3 * 10 * 512 * 512 * HD, 3 * 512 * W * 8),
        name="attend_backward",
    )(near, far, d_near, d_far)


def input_terms(d_proj, weight, n_near, n_far, gain):
    step = 512

    def kernel(d_ref, w_ref, one_ref, two_ref, gain_ref, *outs):
        term = dot_nt(d_ref[0], w_ref[0])
        for s in (1, 2):
            term += dot_nt(d_ref[s], w_ref[s])
        for at in range(8):
            for half in range(2):
                low = 64 * at + 32 * half
                outs[at][half] = term[low : low + 32].astype(BF)
        sums = jnp.sum(term[:256] * one_ref[...].astype(F32), axis=0, keepdims=True)
        sums += jnp.sum(term[256:] * two_ref[...].astype(F32), axis=0, keepdims=True)
        outs[8][...] = sums / gain_ref[...]

    return pl.pallas_call(
        kernel,
        grid=(D // step,),
        in_specs=[
            pl.BlockSpec((3, 512, W), lambda k: (0, 0, 0)),
            pl.BlockSpec((3, step, W), lambda k: (0, k, 0)),
            pl.BlockSpec((256, step), lambda k: (0, k)),
            pl.BlockSpec((256, step), lambda k: (0, k)),
            pl.BlockSpec((1, step), lambda k: (0, k)),
        ],
        out_specs=[pl.BlockSpec((2, 32, step), lambda k: (0, 0, k))] * 8
        + [pl.BlockSpec((1, step), lambda k: (0, k))],
        out_shape=[jax.ShapeDtypeStruct((2, 32, D), BF)] * 8 + [jax.ShapeDtypeStruct((1, D), F32)],
        compiler_params=params(40),
        cost_estimate=cost(2 * 512 * D * 3 * W, 3 * D * W * 2 + 512 * D * 4),
        name="input_terms",
    )(d_proj, weight, n_near, n_far, gain.reshape(1, D))


def weight_terms(blocks, first, count, normed, normed_pair, ups, ups_pair, d_proj, d_pair, att, att_pair):
    def kernel(_, n1, n2, m1, m2, u1, u2, v1, v2, d_ref, e_ref, a_ref, b_ref, out_ref):
        for s in range(3):
            total = dot_tn(n1[...], d_ref[s, :256]) + dot_tn(n2[...], d_ref[s, 256:])
            total += dot_tn(m1[...], e_ref[s, :256]) + dot_tn(m2[...], e_ref[s, 256:])
            out_ref[0, 0, s] = total[:192].astype(BF)
            out_ref[0, 1, s] = total[192:].astype(BF)
        total = dot_tn(a_ref[:256], u1[...]) + dot_tn(a_ref[256:], u2[...])
        total += dot_tn(b_ref[:256], v1[...]) + dot_tn(b_ref[256:], v2[...])
        out_ref[0, 0, 3] = total[:192].astype(BF)
        out_ref[0, 1, 3] = total[192:].astype(BF)

    placed = pl.BlockSpec((256, W), lambda k, b: (0, b[first + k]))
    paired = pl.BlockSpec((256, W), lambda k, b: (0, first + k))
    return pl.pallas_call(
        kernel,
        grid_spec=pltpu.PrefetchScalarGridSpec(
            num_scalar_prefetch=1,
            grid=(count,),
            in_specs=[placed] * 2
            + [paired] * 2
            + [placed] * 2
            + [paired] * 2
            + [pl.BlockSpec((3, 512, W), lambda k, b: (0, 0, 0))] * 2
            + [pl.BlockSpec((512, W), lambda k, b: (0, 0))] * 2,
            out_specs=pl.BlockSpec((1, 2, 4, 192, W), lambda k, b: (k, 0, 0, 0, 0)),
        ),
        out_shape=jax.ShapeDtypeStruct((count, 2, 4, 192, W), BF),
        compiler_params=params(40),
        cost_estimate=cost(count * 2 * 4 * W * W * 1024, count * 4 * W * W * 2 + 4 * 1024 * W * 2),
        name="weight_terms",
    )(blocks, *normed, *normed_pair, *ups, *ups_pair, d_proj, d_pair, att, att_pair)


def body(inputs, upstream, w_qkv, w_out, ln_gain):
    place = lax.axis_index("dp")
    y, zh, core = place // 4, (place // 2) % 2, place % 2
    offsets = [(2, 1), (2, 0), (3, 1), (1, 1), (3, 0), (1, 0), (0, 1), (0, 0)]
    blocks = jnp.stack([(y + dy) % 4 * 4 + (zh ^ dz) * 2 + core for dy, dz in offsets])
    blocks = blocks.astype(jnp.int32)

    in_near, in_far = gather_eight(inputs.reshape(2, 32, D), X_FWD, X_BWD, Z_LOW)
    up_near, up_far = gather_eight(upstream.reshape(2, 32, D), X_FWD, X_BWD, Z_LOW)

    n_near = norm_rows(in_near, ln_gain, near_rows)
    n_far = norm_rows(in_far, ln_gain, far_rows)
    m_near = move(pick_blocks(n_near, blocks ^ 1), CORE)
    m_far = move(pick_blocks(n_far, blocks ^ 1), CORE)
    p_near = project(n_near, w_qkv)
    p_far = project(n_far, w_qkv)
    attended = attend_forward(p_near, p_far)
    att_pair = move(attended, CORE)

    u_near, d_near = upstream_rows(up_near, w_out, near_rows)
    u_far, d_far = upstream_rows(up_far, w_out, far_rows)
    v_near = move(pick_blocks(u_near, blocks ^ 1), CORE)
    v_far = move(pick_blocks(u_far, blocks ^ 1), CORE)

    d_proj = attend_backward(p_near, p_far, d_near, d_far)
    d_pair = move(d_proj, CORE)

    terms = input_terms(d_proj, w_qkv, n_near, n_far, ln_gain)
    own, behind, ahead, across, opposite, a_behind, a_ahead, a_opposite = terms[:8]
    gain_sum = terms[8].reshape(48, 128)
    sums = scatter_eight(
        (terms[0], terms[1], terms[2], terms[3], terms[4], terms[5], terms[6], terms[7]),
        X_FWD,
        X_BWD,
        Z_LOW,
    )

    def weights(first, count):
        out = weight_terms(
            blocks,
            first,
            count,
            (n_near, n_far),
            (m_near, m_far),
            (u_near, u_far),
            (v_near, v_far),
            d_proj,
            d_pair,
            attended,
            att_pair,
        )
        return [out[i] for i in range(count)]

    far = weights(0, 1)
    middle = weights(1, 3)
    near = weights(4, 4)
    weight_sums = scatter_eight(
        (near[3], near[0], near[1], near[2], middle[0], middle[1], middle[2], far[0]),
        Y_FWD,
        Y_BWD,
        Z_HIGH,
    )

    for route in BUTTERFLY:
        gain_sum = gain_sum + move(gain_sum, route)
    grad_gain = gain_sum.reshape(D)

    d_normed = sum(t.astype(F32) for t in sums).reshape(64, D)
    normal, inverse = layer_stats(inputs.astype(F32))
    grad_inputs = (
        upstream.astype(F32) + norm_back(d_normed * ln_gain, normal, inverse)
    ).astype(BF)

    total = sum(t.astype(F32) for t in weight_sums)
    total = total.transpose(1, 0, 2, 3).reshape(4, W, W)
    return (grad_inputs, total[:3], total[3], grad_gain)


def solution(mesh):
    placed = (
        P(("dp", "tensor"), None),
        P(("dp", "tensor"), None),
        P(None, None, "tensor"),
        P("tensor", None),
        P(),
    )
    return jax.shard_map(
        body,
        mesh=mesh,
        in_specs=placed,
        out_specs=(P(("dp", "tensor"), None), P(None, "dp", "tensor"), P("tensor", "dp"), P()),
        check_vma=False,
    )
```

```python
import math

import jax
import jax.numpy as jnp
from jax import lax
from jax.experimental import pallas as pl
from jax.experimental.pallas import tpu as pltpu
from jax.sharding import PartitionSpec as P

HD = 128
EPSILON = 1e-06
D = 6144
W = 384
BF = jnp.bfloat16
F32 = jnp.float32
MIB = 1 << 20
LIMIT_IT = 51
LIMIT_WT = 51
LIMIT_PR = 51

X_FWD = ("tensor", [(z * 4 + x, z * 4 + (x + 1) % 4) for z in range(2) for x in range(4)])
X_BWD = ("tensor", [(z * 4 + x, z * 4 + (x + 3) % 4) for z in range(2) for x in range(4)])
Z_LOW = ("tensor", [(z * 4 + x, (1 - z) * 4 + x) for z in range(2) for x in range(4)])
Y_FWD = ("dp", [(y * 4 + r, (y + 1) % 4 * 4 + r) for y in range(4) for r in range(4)])
Y_BWD = ("dp", [(y * 4 + r, (y + 3) % 4 * 4 + r) for y in range(4) for r in range(4)])
Z_HIGH = ("dp", [(i, i ^ 2) for i in range(16)])
CORE = ("dp", [(i, i ^ 1) for i in range(16)])
BUTTERFLY = [
    CORE,
    Z_HIGH,
    ("dp", [(i, i ^ 4) for i in range(16)]),
    ("dp", [(i, i ^ 8) for i in range(16)]),
    ("tensor", [(i, i ^ 1) for i in range(8)]),
    ("tensor", [(i, i ^ 2) for i in range(8)]),
    Z_LOW,
]


def move(value, route):
    return lax.ppermute(value, route[0], route[1])


def params(limit):
    return pltpu.CompilerParams(vmem_limit_bytes=limit * MIB)


def cost(flops, nbytes):
    return pl.CostEstimate(flops=int(flops), bytes_accessed=int(nbytes), transcendentals=0)


def layer_stats(values):
    average = jnp.mean(values, axis=-1, keepdims=True)
    centered = values - average
    inverse = lax.rsqrt(jnp.mean(centered * centered, axis=-1, keepdims=True) + EPSILON)
    return (centered * inverse, inverse)


def norm_back(grad, normal, inverse):
    return inverse * (
        grad
        - jnp.mean(grad, axis=-1, keepdims=True)
        - normal * jnp.mean(grad * normal, axis=-1, keepdims=True)
    )


def after(value, *others):
    return lax.optimization_barrier((value, others))[0]


def gather_stacks(near):
    _, behind, ahead, across = near
    return (
        jnp.stack([behind[0], across[0]]),
        jnp.stack([ahead[1], across[1]]),
        jnp.stack([behind[1], ahead[0]]),
    )


def gather_first(own, *before_swap):
    return (own, move(own, X_FWD), move(own, X_BWD), move(after(own, *before_swap), Z_LOW))


def gather_second(stacks):
    return tuple(move(s, route) for s, route in zip(stacks, (X_FWD, X_BWD, Z_LOW)))


def gather_third(pieces):
    return (move(pieces[0], X_FWD), move(pieces[1], X_BWD))


def near_rows(refs):
    return [r[i] for r in refs for i in range(2)]


def far_rows(refs):
    fb, fa, fz, lt, lb = refs
    return [fb[0], fa[0], fb[1], fz[0], fz[1], fa[1], lt[...], lb[...]]


def add(a, b):
    return (a.astype(F32) + b.astype(F32)).astype(BF)


def halves(top, bottom):
    return jnp.stack([top, bottom])


def norm_rows(pieces, gain, picker):
    def kernel(*refs):
        gain_ref, out_ref = refs[-2:]
        for at, rows in enumerate(picker(refs[:-2])):
            normal, _ = layer_stats(rows.astype(F32))
            out_ref[32 * at : 32 * at + 32, :] = (normal * gain_ref[...]).astype(BF)

    return pl.pallas_call(
        kernel,
        out_shape=jax.ShapeDtypeStruct((256, D), BF),
        compiler_params=params(20),
        cost_estimate=cost(256 * D * 10, 256 * D * 4),
        name="norm_rows",
    )(*pieces, gain.reshape(1, D))


def wide(ref):
    return jnp.concatenate([ref[0], ref[1], ref[2]], axis=1)


def project_rows(normed, weight):
    step = 1536

    def kernel(x_ref, w_ref, out_ref):
        @pl.when(pl.program_id(0) == 0)
        def _():
            out_ref[...] = jnp.zeros_like(out_ref)

        out_ref[...] += jnp.dot(x_ref[...], wide(w_ref), preferred_element_type=F32)

    return pl.pallas_call(
        kernel,
        grid=(D // step,),
        in_specs=[
            pl.BlockSpec((256, step), lambda k: (0, k)),
            pl.BlockSpec((3, step, W), lambda k: (0, k, 0)),
        ],
        out_specs=pl.BlockSpec((256, 3 * W), lambda k: (0, 0)),
        out_shape=jax.ShapeDtypeStruct((256, 3 * W), F32),
        compiler_params=params(LIMIT_PR),
        cost_estimate=cost(2 * 256 * D * 3 * W, 3 * D * W * 2 + 256 * D * 2),
        name="project_rows",
    )(normed, weight)


def upstream_rows(pieces, w_out, picker):
    step = 1536

    def kernel(*refs):
        w_ref, cat_ref, out_ref, acc = refs[-4:]
        k = pl.program_id(0)

        @pl.when(k == 0)
        def _():
            acc[...] = jnp.zeros_like(acc)

        for at, rows in enumerate(picker(refs[:-4])):
            cat_ref[32 * at : 32 * at + 32, :] = rows
        acc[...] += dot_nt(cat_ref[...], w_ref[...])

        @pl.when(k == D // step - 1)
        def _():
            out_ref[...] = acc[...].astype(BF)

    specs = [
        pl.BlockSpec((2, 32, step), lambda k: (0, 0, k))
        if piece.ndim == 3
        else pl.BlockSpec((32, step), lambda k: (0, k))
        for piece in pieces
    ]
    return pl.pallas_call(
        kernel,
        grid=(D // step,),
        in_specs=specs + [pl.BlockSpec((W, step), lambda k: (0, k))],
        out_specs=[
            pl.BlockSpec((256, step), lambda k: (0, k)),
            pl.BlockSpec((256, W), lambda k: (0, 0)),
        ],
        out_shape=[jax.ShapeDtypeStruct((256, D), BF), jax.ShapeDtypeStruct((256, W), BF)],
        scratch_shapes=[pltpu.VMEM((256, W), F32)],
        compiler_params=params(20),
        cost_estimate=cost(2 * 256 * D * W, D * W * 2 + 256 * D * 4),
        name="upstream_rows",
    )(*pieces, w_out)


SCALE = 1.0 / math.sqrt(HD)


def dot_nt(a, b):
    return lax.dot_general(a, b, (((1,), (1,)), ((), ())), preferred_element_type=F32)


def dot_tn(a, b):
    return lax.dot_general(a, b, (((0,), (0,)), ((), ())), preferred_element_type=F32)


def dot_nn(a, b):
    return jnp.dot(a, b, preferred_element_type=F32)


def join(refs):
    return jnp.concatenate([r[...] for r in refs], axis=0)


def head_specs():
    return [
        pl.BlockSpec((256, HD), lambda h, s=s: (0, s * (W // HD) + h)) for s in range(3) for _ in range(2)
    ]


def attend_forward(near, far):
    def kernel(q1, q2, k1, k2, v1, v2, out_ref):
        query, _ = layer_stats(join((q1, q2)))
        key, _ = layer_stats(join((k1, k2)))
        value = join((v1, v2)).astype(BF)
        exponent = jnp.exp(dot_nt(query.astype(BF), key.astype(BF)) * SCALE)
        attention = exponent / jnp.sum(exponent, axis=-1, keepdims=True)
        out_ref[...] = dot_nn(attention.astype(BF), value).astype(BF)

    return pl.pallas_call(
        kernel,
        grid=(W // HD,),
        in_specs=head_specs(),
        out_specs=pl.BlockSpec((512, HD), lambda h: (0, h)),
        out_shape=jax.ShapeDtypeStruct((512, W), BF),
        compiler_params=params(40),
        cost_estimate=cost(3 * 4 * 512 * 512 * HD, 3 * 512 * W * 4),
        name="attend_forward",
    )(*(near, far) * 3)


def attend_backward(near, far, d_near, d_far):
    def kernel(q1, q2, k1, k2, v1, v2, d1, d2, out_ref):
        def put(s, values):
            column = pl.multiple_of(s * W + pl.program_id(0) * HD, HD)
            out_ref[:, pl.ds(column, HD)] = values.astype(BF)

        query, query_inv = layer_stats(join((q1, q2)))
        key, key_inv = layer_stats(join((k1, k2)))
        value_low = join((v1, v2)).astype(BF)
        query_low = query.astype(BF)
        key_low = key.astype(BF)
        d_att = join((d1, d2))
        exponent = jnp.exp(dot_nt(query_low, key_low) * SCALE)
        attention = exponent / jnp.sum(exponent, axis=-1, keepdims=True)
        d_raw = dot_nt(d_att, value_low)
        put(2, dot_tn(attention.astype(BF), d_att))
        inner = jnp.sum(d_raw * attention, axis=-1, keepdims=True)
        d_scores = (attention * (d_raw - inner) * SCALE).astype(BF)
        put(0, norm_back(dot_nn(d_scores, key_low), query, query_inv))
        put(1, norm_back(dot_tn(d_scores, query_low), key, key_inv))

    return pl.pallas_call(
        kernel,
        grid=(W // HD,),
        in_specs=head_specs() + [pl.BlockSpec((256, HD), lambda h: (0, h))] * 2,
        out_specs=pl.BlockSpec((512, 3 * W), lambda h: (0, 0)),
        out_shape=jax.ShapeDtypeStruct((512, 3 * W), BF),
        compiler_params=params(48),
        cost_estimate=cost(3 * 10 * 512 * 512 * HD, 3 * 512 * W * 8),
        name="attend_backward",
    )(*(near, far) * 3, d_near, d_far)


def input_terms(d_proj, weight, n_near, n_far, gain):
    step = 1024
    far = {(4, 0): (4, 0), (5, 0): (4, 1), (5, 1): (4, 2), (4, 1): (5, 0), (6, 0): (5, 1), (6, 1): (5, 2)}

    def kernel(d_ref, w_ref, n1, n2, gain_ref, *outs):
        term = dot_nt(d_ref[...], wide(w_ref))
        for at in range(8):
            for half in range(2):
                low = 64 * at + 32 * half
                rows = term[low : low + 32].astype(BF)
                if at < 4:
                    outs[at][half] = rows
                elif at < 7:
                    out, row = far[at, half]
                    outs[out][row] = rows
                else:
                    outs[6 + half][...] = rows
        sums = jnp.sum(term * join((n1, n2)).astype(F32), axis=0, keepdims=True)
        outs[8][...] = sums / gain_ref[...]

    return pl.pallas_call(
        kernel,
        grid=(D // step,),
        in_specs=[
            pl.BlockSpec((512, 3 * W), lambda k: (0, 0)),
            pl.BlockSpec((3, step, W), lambda k: (0, k, 0)),
            pl.BlockSpec((256, step), lambda k: (0, k)),
            pl.BlockSpec((256, step), lambda k: (0, k)),
            pl.BlockSpec((1, step), lambda k: (0, k)),
        ],
        out_specs=[pl.BlockSpec((2, 32, step), lambda k: (0, 0, k))] * 4
        + [pl.BlockSpec((3, 32, step), lambda k: (0, 0, k))] * 2
        + [pl.BlockSpec((32, step), lambda k: (0, k))] * 2
        + [pl.BlockSpec((1, step), lambda k: (0, k))],
        out_shape=[jax.ShapeDtypeStruct((2, 32, D), BF)] * 4
        + [jax.ShapeDtypeStruct((3, 32, D), BF)] * 2
        + [jax.ShapeDtypeStruct((32, D), BF)] * 2
        + [jax.ShapeDtypeStruct((1, D), F32)],
        compiler_params=params(LIMIT_IT),
        cost_estimate=cost(2 * 512 * D * 3 * W, 3 * D * W * 2 + 512 * D * 4),
        name="input_terms",
    )(d_proj, weight, n_near, n_far, gain.reshape(1, D))


def weight_terms(blocks, first, count, operands):
    def kernel(_, n1, n2, m1, m2, u1, u2, v1, v2, d_ref, e_ref, a_ref, b_ref, *outs):
        total = dot_tn(join((n1, n2)), d_ref[...]) + dot_tn(join((m1, m2)), e_ref[...])
        total = total.astype(BF)
        other = dot_tn(a_ref[...], join((u1, u2))) + dot_tn(b_ref[...], join((v1, v2)))
        other = other.astype(BF)

        def put(half, place):
            low = 192 * half
            for s in range(3):
                place(s, total[low : low + 192, s * W : (s + 1) * W])
            place(3, other[low : low + 192])

        def put_in(half, ref, index):
            def place(s, values):
                ref[index + (s,)] = values

            put(half, place)

        if count == 1:
            put_in(0, outs[0], ())
            put_in(1, outs[1], ())
        elif count == 4:
            put_in(0, outs[0], (0, 0))
            put_in(1, outs[0], (0, 1))
        else:
            back, forth, across = outs
            for k, (top, bottom) in enumerate(
                [((back, 0), (forth, 0)), ((back, 1), (across, 0)), ((across, 1), (forth, 1))]
            ):

                @pl.when(pl.program_id(0) == k)
                def _():
                    put_in(0, top[0], (top[1],))
                    put_in(1, bottom[0], (bottom[1],))

    placed = pl.BlockSpec((256, W), lambda k, b: (0, b[first + k]))
    flat = pl.BlockSpec((512, 3 * W), lambda k, b: (0, 0))
    narrow = pl.BlockSpec((512, W), lambda k, b: (0, 0))
    if count == 1:
        shapes = [(4, 192, W)] * 2
    elif count == 3:
        shapes = [(2, 4, 192, W)] * 3
    else:
        shapes = [(count, 2, 4, 192, W)]
    if count == 4:
        specs = [pl.BlockSpec((1, 2, 4, 192, W), lambda k, b: (k, 0, 0, 0, 0))]
    else:
        specs = [pl.BlockSpec(shape, lambda k, b, n=len(shape): (0,) * n) for shape in shapes]
    return pl.pallas_call(
        kernel,
        grid_spec=pltpu.PrefetchScalarGridSpec(
            num_scalar_prefetch=1,
            grid=(count,),
            in_specs=[placed] * 8 + [flat, flat, narrow, narrow],
            out_specs=specs,
        ),
        out_shape=[jax.ShapeDtypeStruct(shape, BF) for shape in shapes],
        compiler_params=params(LIMIT_WT),
        cost_estimate=cost(count * 8 * W * W * 1024, count * 4 * W * W * 2 + 4 * 1024 * W * 2),
        name="weight_terms",
    )(blocks, *operands)


def body(inputs, upstream, w_qkv, w_out, ln_gain):
    place = lax.axis_index("dp")
    y, zh, core = place // 4, (place // 2) % 2, place % 2
    offsets = [(2, 1), (2, 0), (3, 1), (1, 1), (3, 0), (1, 0), (0, 1), (0, 0)]
    blocks = jnp.stack([(y + dy) % 4 * 4 + (zh ^ dz) * 2 + core for dy, dz in offsets])
    blocks = blocks.astype(jnp.int32)

    in_near = gather_first(inputs.reshape(2, 32, D))
    in_stacks = gather_stacks(in_near)
    in_second = gather_second(in_stacks)
    up_near = gather_first(after(upstream.reshape(2, 32, D), in_stacks), in_second)

    n_near = norm_rows(in_near, ln_gain, near_rows)
    pair_n_near = move(n_near, CORE)
    p_near = project_rows(n_near, w_qkv)

    in_second = after(in_second, p_near)
    in_third = gather_third((in_second[0][1], in_second[1][1]))
    up_stacks = gather_stacks(after(up_near, in_third))
    up_second = gather_second(up_stacks)

    u_near, d_near = upstream_rows(after(up_near, up_stacks), w_out, near_rows)
    pair_u_near = move(u_near, CORE)
    n_far = norm_rows(after(in_second + in_third, d_near, pair_n_near), ln_gain, far_rows)
    pair_n_far = move(n_far, CORE)
    p_far = project_rows(after(n_far, pair_u_near), w_qkv)
    attended = attend_forward(p_near, p_far)
    pair_attended = move(attended, CORE)

    up_second = after(up_second, attended, pair_n_far)
    up_third = gather_third((up_second[0][1], up_second[1][1]))
    u_far, d_far = upstream_rows(after(up_second + up_third, pair_attended), w_out, far_rows)
    pair_u_far = move(u_far, CORE)
    d_proj = attend_backward(p_near, p_far, d_near, d_far)
    pair_d = move(d_proj, CORE)

    def exchange(value, step):
        return value + move(value, BUTTERFLY[step])

    *rows, gain_sum = input_terms(after(d_proj, pair_u_far), w_qkv, n_near, n_far, ln_gain)
    gain_sum = exchange(gain_sum.reshape(48, 128), 0)
    own, behind, ahead, across, back, forth, top, bottom = after(tuple(rows), pair_d)
    by_back, by_forth = move(top, X_BWD), move(bottom, X_FWD)

    operands = (n_near, n_far, pair_n_near, pair_n_far, u_near, u_far, pair_u_near, pair_u_far)
    operands += (d_proj, pair_d, attended, pair_attended)
    far = weight_terms(blocks, 0, 1, after(operands, gain_sum))
    gain_sum = exchange(gain_sum, 1)
    g_top, g_bottom = after(far, gain_sum)
    g_by_back, g_by_forth = move(g_top, Y_BWD), move(g_bottom, Y_FWD)
    gain_sum = exchange(gain_sum, 2)
    g_back, g_forth, g_across = weight_terms(blocks, 1, 3, after(operands, far))
    g_by_across = move(g_across, Z_HIGH)

    back, forth, by_back, by_forth = after((back, forth, by_back, by_forth), g_across, gain_sum)
    back = back.at[1].set(add(back[1], by_back))
    forth = forth.at[2].set(add(forth[2], by_forth))
    by_back, by_forth = move(back, X_BWD), move(forth, X_FWD)
    gain_sum = exchange(after(gain_sum, back, forth), 3)

    g_by_back, g_by_forth = after((g_by_back, g_by_forth), back, forth)
    g_back = g_back.at[1].set(add(g_back[1], g_by_back))
    g_forth = g_forth.at[1].set(add(g_forth[1], g_by_forth))
    g_back, g_forth = after((g_back, g_forth), gain_sum)
    g_by_back, g_by_forth = move(g_back, Y_BWD), move(g_forth, Y_FWD)
    (near,) = weight_terms(blocks, 4, 4, after(operands, g_back, g_forth))

    by_back, by_forth, g_by_across = after((by_back, by_forth, g_by_across), near)
    behind = behind.at[0].set(add(behind[0], by_back[0]))
    ahead = ahead.at[1].set(add(ahead[1], by_forth[0]))
    across = (across.astype(F32) + by_back[1:].astype(F32) + by_forth[1:].astype(F32)).astype(BF)
    by_behind, by_ahead = move(behind, X_BWD), move(ahead, X_FWD)

    g_by_back, g_by_forth = after((g_by_back, g_by_forth), behind, ahead, across)
    g_behind = add(near[0], halves(g_by_back[0], g_by_across[0]))
    g_ahead = add(near[1], halves(g_by_across[1], g_by_forth[0]))
    g_over = add(near[2], halves(g_by_back[1], g_by_forth[1]))
    g_terms = (near[3], move(g_behind, Y_BWD), move(g_ahead, Y_FWD), move(g_over, Z_HIGH))

    by_across = move(after(across, by_behind, by_ahead, g_behind, g_ahead, g_over), Z_LOW)
    gain_sum = after(gain_sum, by_behind, by_ahead)
    for step in (4, 5, 6):
        gain_sum = exchange(gain_sum, step)
    grad_gain = gain_sum.reshape(D)

    terms = (own, by_behind, by_ahead, by_across)
    d_normed = sum(t.astype(F32) for t in terms).reshape(64, D)
    normal, inverse = layer_stats(inputs.astype(F32))
    grad_inputs = (
        upstream.astype(F32) + norm_back(d_normed * ln_gain, normal, inverse)
    ).astype(BF)

    total = sum(t.astype(F32) for t in g_terms)
    total = total.transpose(1, 0, 2, 3).reshape(4, W, W)
    return (grad_inputs, total[:3], total[3], grad_gain)


def solution(mesh):
    placed = (
        P(("dp", "tensor"), None),
        P(("dp", "tensor"), None),
        P(None, None, "tensor"),
        P("tensor", None),
        P(),
    )
    return jax.shard_map(
        body,
        mesh=mesh,
        in_specs=placed,
        out_specs=(P(("dp", "tensor"), None), P(None, "dp", "tensor"), P("tensor", "dp"), P()),
        check_vma=False,
    )
```

```python
import math

import jax
import jax.numpy as jnp
from jax import lax
from jax.experimental import pallas as pl
from jax.experimental.pallas import tpu as pltpu
from jax.sharding import PartitionSpec as P

HD = 128
EPSILON = 1e-06
D = 6144
W = 384
BF = jnp.bfloat16
F32 = jnp.float32
MIB = 1 << 20
LIMIT_IT = 51
LIMIT_WT = 51
LIMIT_PR = 51
SHARE = 20

X_FWD = ("tensor", [(z * 4 + x, z * 4 + (x + 1) % 4) for z in range(2) for x in range(4)])
X_BWD = ("tensor", [(z * 4 + x, z * 4 + (x + 3) % 4) for z in range(2) for x in range(4)])
Z_LOW = ("tensor", [(z * 4 + x, (1 - z) * 4 + x) for z in range(2) for x in range(4)])
Y_FWD = ("dp", [(y * 4 + r, (y + 1) % 4 * 4 + r) for y in range(4) for r in range(4)])
Y_BWD = ("dp", [(y * 4 + r, (y + 3) % 4 * 4 + r) for y in range(4) for r in range(4)])
Z_HIGH = ("dp", [(i, i ^ 2) for i in range(16)])
CORE = ("dp", [(i, i ^ 1) for i in range(16)])
BUTTERFLY = [
    CORE,
    Z_HIGH,
    ("dp", [(i, i ^ 4) for i in range(16)]),
    ("dp", [(i, i ^ 8) for i in range(16)]),
    Z_LOW,
    ("tensor", [(i, i ^ 1) for i in range(8)]),
    ("tensor", [(i, i ^ 2) for i in range(8)]),
]


def move(value, route):
    return lax.ppermute(value, route[0], route[1])


def params(limit):
    return pltpu.CompilerParams(vmem_limit_bytes=limit * MIB)


def cost(flops, nbytes):
    return pl.CostEstimate(flops=int(flops) // SHARE, bytes_accessed=int(nbytes) // SHARE, transcendentals=0)


def layer_stats(values):
    average = jnp.mean(values, axis=-1, keepdims=True)
    centered = values - average
    inverse = lax.rsqrt(jnp.mean(centered * centered, axis=-1, keepdims=True) + EPSILON)
    return (centered * inverse, inverse)


def norm_back(grad, normal, inverse):
    return inverse * (
        grad
        - jnp.mean(grad, axis=-1, keepdims=True)
        - normal * jnp.mean(grad * normal, axis=-1, keepdims=True)
    )


def after(value, *others):
    return lax.optimization_barrier((value, others))[0]


def gather_stacks(near):
    _, behind, ahead, across = near
    return (
        jnp.stack([behind[0], across[0]]),
        jnp.stack([ahead[1], across[1]]),
        jnp.stack([behind[1], ahead[0]]),
    )


def gather_first(own, *before_swap):
    return (own, move(own, X_FWD), move(own, X_BWD), move(after(own, *before_swap), Z_LOW))


def gather_second(stacks):
    return tuple(move(s, route) for s, route in zip(stacks, (X_FWD, X_BWD, Z_LOW)))


def gather_third(pieces):
    return (move(pieces[0], X_FWD), move(pieces[1], X_BWD))


def near_rows(refs):
    return [r[i] for r in refs for i in range(2)]


def middle_rows(refs):
    fb, fa, fz = refs
    return [fb[0], fa[0], fb[1], fz[0], fz[1], fa[1]]


def last_rows(refs):
    return [r[...] for r in refs]


def far_rows(refs):
    return middle_rows(refs[:3]) + last_rows(refs[3:])


def add(a, b):
    return (a.astype(F32) + b.astype(F32)).astype(BF)


def halves(top, bottom):
    return jnp.stack([top, bottom])


def add_at(*sums):
    def kernel(*refs):
        count = len(sums)
        for values, term, out in zip(refs[:count], refs[count : 2 * count], refs[2 * count :]):
            out[0] = add(values[0], term[...])

    def placed(values, index):
        zeros = (0,) * (values.ndim - 1)
        return pl.BlockSpec((1,) + values.shape[1:], lambda i: (index,) + zeros)

    def whole(term):
        return pl.BlockSpec(term.shape, lambda i: (0,) * term.ndim)

    spots = [placed(values, index) for values, index, _ in sums]
    return pl.pallas_call(
        kernel,
        grid=(1,),
        in_specs=spots + [whole(term) for _, _, term in sums],
        out_specs=spots,
        out_shape=[jax.ShapeDtypeStruct(values.shape, BF) for values, _, _ in sums],
        input_output_aliases={i: i for i in range(len(sums))},
        compiler_params=params(LIMIT_PR),
        cost_estimate=cost(0, sum(term.size * 6 for _, _, term in sums)),
        name="add_at",
    )(*(values for values, _, _ in sums), *(term for _, _, term in sums))


def norm_rows(pieces, gain, picker):
    def kernel(*refs):
        gain_ref, out_ref = refs[-2:]
        for at, rows in enumerate(picker(refs[:-2])):
            normal, _ = layer_stats(rows.astype(F32))
            out_ref[32 * at : 32 * at + 32, :] = (normal * gain_ref[...]).astype(BF)

    return pl.pallas_call(
        kernel,
        out_shape=jax.ShapeDtypeStruct((256, D), BF),
        compiler_params=params(20),
        cost_estimate=cost(256 * D * 10, 256 * D * 4),
        name="norm_rows",
    )(*pieces, gain.reshape(1, D))


def wide(ref):
    return jnp.concatenate([ref[0], ref[1], ref[2]], axis=1)


def project_rows(normed, weight):
    step = 1536

    def kernel(x_ref, w_ref, out_ref):
        @pl.when(pl.program_id(0) == 0)
        def _():
            out_ref[...] = jnp.zeros_like(out_ref)

        out_ref[...] += jnp.dot(x_ref[...], wide(w_ref), preferred_element_type=F32)

    return pl.pallas_call(
        kernel,
        grid=(D // step,),
        in_specs=[
            pl.BlockSpec((256, step), lambda k: (0, k)),
            pl.BlockSpec((3, step, W), lambda k: (0, k, 0)),
        ],
        out_specs=pl.BlockSpec((256, 3 * W), lambda k: (0, 0)),
        out_shape=jax.ShapeDtypeStruct((256, 3 * W), F32),
        compiler_params=params(LIMIT_PR),
        cost_estimate=cost(2 * 256 * D * 3 * W, 3 * D * W * 2 + 256 * D * 2),
        name="project_rows",
    )(normed, weight)


def upstream_rows(pieces, w_out, picker):
    step = 1536
    size = sum(piece.size for piece in pieces) // D

    def kernel(*refs):
        w_ref, cat_ref, out_ref, acc = refs[-4:]
        k = pl.program_id(0)

        @pl.when(k == 0)
        def _():
            acc[...] = jnp.zeros_like(acc)

        for at, rows in enumerate(picker(refs[:-4])):
            cat_ref[32 * at : 32 * at + 32, :] = rows
        acc[...] += dot_nt(cat_ref[...], w_ref[...])

        @pl.when(k == D // step - 1)
        def _():
            out_ref[...] = acc[...].astype(BF)

    specs = [
        pl.BlockSpec((2, 32, step), lambda k: (0, 0, k))
        if piece.ndim == 3
        else pl.BlockSpec((32, step), lambda k: (0, k))
        for piece in pieces
    ]
    return pl.pallas_call(
        kernel,
        grid=(D // step,),
        in_specs=specs + [pl.BlockSpec((W, step), lambda k: (0, k))],
        out_specs=[
            pl.BlockSpec((size, step), lambda k: (0, k)),
            pl.BlockSpec((size, W), lambda k: (0, 0)),
        ],
        out_shape=[jax.ShapeDtypeStruct((size, D), BF), jax.ShapeDtypeStruct((size, W), BF)],
        scratch_shapes=[pltpu.VMEM((size, W), F32)],
        compiler_params=params(LIMIT_PR),
        cost_estimate=cost(2 * size * D * W, D * W * 2 + size * D * 4),
        name="upstream_rows",
    )(*pieces, w_out)


SCALE = 1.0 / math.sqrt(HD)


def dot_nt(a, b):
    return lax.dot_general(a, b, (((1,), (1,)), ((), ())), preferred_element_type=F32)


def dot_tn(a, b):
    return lax.dot_general(a, b, (((0,), (0,)), ((), ())), preferred_element_type=F32)


def dot_nn(a, b):
    return jnp.dot(a, b, preferred_element_type=F32)


def join(refs):
    return jnp.concatenate([r[...] for r in refs], axis=0)


def head_specs():
    return [
        pl.BlockSpec((256, HD), lambda h, s=s: (0, s * (W // HD) + h)) for s in range(3) for _ in range(2)
    ]


def attend_forward(near, far):
    def kernel(q1, q2, k1, k2, v1, v2, out_ref):
        query, _ = layer_stats(join((q1, q2)))
        key, _ = layer_stats(join((k1, k2)))
        value = join((v1, v2)).astype(BF)
        exponent = jnp.exp(dot_nt(query.astype(BF), key.astype(BF)) * SCALE)
        attention = exponent / jnp.sum(exponent, axis=-1, keepdims=True)
        out_ref[...] = dot_nn(attention.astype(BF), value).astype(BF)

    return pl.pallas_call(
        kernel,
        grid=(W // HD,),
        in_specs=head_specs(),
        out_specs=pl.BlockSpec((512, HD), lambda h: (0, h)),
        out_shape=jax.ShapeDtypeStruct((512, W), BF),
        compiler_params=params(40),
        cost_estimate=cost(3 * 4 * 512 * 512 * HD, 3 * 512 * W * 4),
        name="attend_forward",
    )(*(near, far) * 3)


def attend_backward(near, far, *d_pieces):
    def kernel(q1, q2, k1, k2, v1, v2, d1, d2, d3, out_ref):
        def put(s, values):
            column = pl.multiple_of(s * W + pl.program_id(0) * HD, HD)
            out_ref[:, pl.ds(column, HD)] = values.astype(BF)

        query, query_inv = layer_stats(join((q1, q2)))
        key, key_inv = layer_stats(join((k1, k2)))
        value_low = join((v1, v2)).astype(BF)
        query_low = query.astype(BF)
        key_low = key.astype(BF)
        d_att = join((d1, d2, d3))
        exponent = jnp.exp(dot_nt(query_low, key_low) * SCALE)
        attention = exponent / jnp.sum(exponent, axis=-1, keepdims=True)
        d_raw = dot_nt(d_att, value_low)
        put(2, dot_tn(attention.astype(BF), d_att))
        inner = jnp.sum(d_raw * attention, axis=-1, keepdims=True)
        d_scores = (attention * (d_raw - inner) * SCALE).astype(BF)
        put(0, norm_back(dot_nn(d_scores, key_low), query, query_inv))
        put(1, norm_back(dot_tn(d_scores, query_low), key, key_inv))

    return pl.pallas_call(
        kernel,
        grid=(W // HD,),
        in_specs=head_specs() + [pl.BlockSpec((d.shape[0], HD), lambda h: (0, h)) for d in d_pieces],
        out_specs=pl.BlockSpec((512, 3 * W), lambda h: (0, 0)),
        out_shape=jax.ShapeDtypeStruct((512, 3 * W), BF),
        compiler_params=params(48),
        cost_estimate=cost(3 * 10 * 512 * 512 * HD, 3 * 512 * W * 8),
        name="attend_backward",
    )(*(near, far) * 3, *d_pieces)


def input_terms(d_proj, weight, n_near, n_far, gain):
    step = 1024
    far = {(4, 0): (4, 0), (5, 0): (4, 1), (5, 1): (4, 2), (4, 1): (5, 0), (6, 0): (5, 1), (6, 1): (5, 2)}

    def kernel(d_ref, w_ref, n1, n2, gain_ref, *outs):
        term = dot_nt(d_ref[...], wide(w_ref))
        for at in range(8):
            for half in range(2):
                low = 64 * at + 32 * half
                rows = term[low : low + 32].astype(BF)
                if at < 4:
                    outs[at][half] = rows
                elif at < 7:
                    out, row = far[at, half]
                    outs[out][row] = rows
                else:
                    outs[6 + half][...] = rows
        sums = jnp.sum(term * join((n1, n2)).astype(F32), axis=0, keepdims=True)
        outs[8][...] = sums / gain_ref[...]

    return pl.pallas_call(
        kernel,
        grid=(D // step,),
        in_specs=[
            pl.BlockSpec((512, 3 * W), lambda k: (0, 0)),
            pl.BlockSpec((3, step, W), lambda k: (0, k, 0)),
            pl.BlockSpec((256, step), lambda k: (0, k)),
            pl.BlockSpec((256, step), lambda k: (0, k)),
            pl.BlockSpec((1, step), lambda k: (0, k)),
        ],
        out_specs=[pl.BlockSpec((2, 32, step), lambda k: (0, 0, k))] * 4
        + [pl.BlockSpec((3, 32, step), lambda k: (0, 0, k))] * 2
        + [pl.BlockSpec((32, step), lambda k: (0, k))] * 2
        + [pl.BlockSpec((1, step), lambda k: (0, k))],
        out_shape=[jax.ShapeDtypeStruct((2, 32, D), BF)] * 4
        + [jax.ShapeDtypeStruct((3, 32, D), BF)] * 2
        + [jax.ShapeDtypeStruct((32, D), BF)] * 2
        + [jax.ShapeDtypeStruct((1, D), F32)],
        compiler_params=params(LIMIT_IT),
        cost_estimate=cost(2 * 512 * D * 3 * W, 3 * D * W * 2 + 512 * D * 4),
        name="input_terms",
    )(d_proj, weight, n_near, n_far, gain.reshape(1, D))


def weight_terms(blocks, first, count, operands):
    def kernel(_, n1, n2, m1, m2, u1, u2, u3, v1, v2, v3, d_ref, e_ref, a_ref, b_ref, *outs):
        total = dot_tn(join((n1, n2)), d_ref[...]) + dot_tn(join((m1, m2)), e_ref[...])
        total = total.astype(BF)
        other = dot_tn(a_ref[...], join((u1, u2, u3))) + dot_tn(b_ref[...], join((v1, v2, v3)))
        other = other.astype(BF)

        def put(half, place):
            low = 192 * half
            for s in range(3):
                place(s, total[low : low + 192, s * W : (s + 1) * W])
            place(3, other[low : low + 192])

        def put_in(half, ref, index):
            def place(s, values):
                ref[index + (s,)] = values

            put(half, place)

        if count == 1:
            put_in(0, outs[0], ())
            put_in(1, outs[1], ())
        elif count == 4:
            put_in(0, outs[0], (0, 0))
            put_in(1, outs[0], (0, 1))
        else:
            back, forth, across = outs
            for k, (top, bottom) in enumerate(
                [((back, 0), (forth, 0)), ((back, 1), (across, 0)), ((across, 1), (forth, 1))]
            ):

                @pl.when(pl.program_id(0) == k)
                def _():
                    put_in(0, top[0], (top[1],))
                    put_in(1, bottom[0], (bottom[1],))

    placed = [
        pl.BlockSpec((rows.shape[0], W), lambda k, b: (0, b[first + k])) for rows in operands[:10]
    ]
    flat = pl.BlockSpec((512, 3 * W), lambda k, b: (0, 0))
    narrow = pl.BlockSpec((512, W), lambda k, b: (0, 0))
    if count == 1:
        shapes = [(4, 192, W)] * 2
    elif count == 3:
        shapes = [(2, 4, 192, W)] * 3
    else:
        shapes = [(count, 2, 4, 192, W)]
    if count == 4:
        specs = [pl.BlockSpec((1, 2, 4, 192, W), lambda k, b: (k, 0, 0, 0, 0))]
    else:
        specs = [pl.BlockSpec(shape, lambda k, b, n=len(shape): (0,) * n) for shape in shapes]
    return pl.pallas_call(
        kernel,
        grid_spec=pltpu.PrefetchScalarGridSpec(
            num_scalar_prefetch=1,
            grid=(count,),
            in_specs=placed + [flat, flat, narrow, narrow],
            out_specs=specs,
        ),
        out_shape=[jax.ShapeDtypeStruct(shape, BF) for shape in shapes],
        compiler_params=params(LIMIT_WT),
        cost_estimate=cost(count * 8 * W * W * 1024, count * 4 * W * W * 2 + 4 * 1024 * W * 2),
        name="weight_terms",
    )(blocks, *operands)


def weight_sums(terms):
    def kernel(own, *refs):
        qkv_ref, out_ref = refs[-2:]
        for half in range(2):
            for s in range(4):
                total = own[0, half, s].astype(F32)
                for ref in refs[:3]:
                    total += ref[half, s].astype(F32)
                if s < 3:
                    qkv_ref[s, 192 * half : 192 * half + 192, :] = total
                else:
                    out_ref[192 * half : 192 * half + 192, :] = total

    near, *others = terms
    whole = pl.BlockSpec((2, 4, 192, W), lambda i: (0, 0, 0, 0))
    return pl.pallas_call(
        kernel,
        grid=(1,),
        in_specs=[pl.BlockSpec((1, 2, 4, 192, W), lambda i: (3, 0, 0, 0, 0))] + [whole] * 3,
        out_specs=[
            pl.BlockSpec((3, W, W), lambda i: (0, 0, 0)),
            pl.BlockSpec((W, W), lambda i: (0, 0)),
        ],
        out_shape=[jax.ShapeDtypeStruct((3, W, W), F32), jax.ShapeDtypeStruct((W, W), F32)],
        compiler_params=params(24),
        cost_estimate=cost(16 * W * W, 4 * 4 * W * W * 3),
        name="weight_sums",
    )(near, *others)


def body(inputs, upstream, w_qkv, w_out, ln_gain):
    place = lax.axis_index("dp")
    y, zh, core = place // 4, (place // 2) % 2, place % 2
    offsets = [(2, 1), (2, 0), (3, 1), (1, 1), (3, 0), (1, 0), (0, 1), (0, 0)]
    blocks = jnp.stack([(y + dy) % 4 * 4 + (zh ^ dz) * 2 + core for dy, dz in offsets])
    blocks = blocks.astype(jnp.int32)

    in_near = gather_first(inputs.reshape(2, 32, D))
    in_stacks = gather_stacks(in_near)
    in_second = gather_second(in_stacks)
    up_near = gather_first(after(upstream.reshape(2, 32, D), in_stacks), in_second)

    n_near = norm_rows(in_near, ln_gain, near_rows)
    p_near = project_rows(n_near, w_qkv)

    in_second = after(in_second, p_near)
    in_third = gather_third((in_second[0][1], in_second[1][1]))
    up_stacks = gather_stacks(after(up_near, in_third))
    up_second = gather_second(up_stacks)

    n_far = norm_rows(after(in_second + in_third, up_stacks), ln_gain, far_rows)
    p_far = project_rows(n_far, w_qkv)
    u_near, d_near = upstream_rows(after(up_near, p_far), w_out, near_rows)
    attended = attend_forward(p_near, after(p_far, d_near))

    up_second = after(up_second, attended)
    up_pieces = (up_second[0][1], up_second[1][1])
    up_third = gather_third(up_pieces)
    u_mid, d_mid = upstream_rows(after(up_second, up_pieces), w_out, middle_rows)
    up_third = after(up_third, d_mid)

    pair_n_near, pair_n_far, pair_attended = (
        move(values, CORE) for values in after((n_near, n_far, attended), up_third)
    )
    u_last, d_last = upstream_rows(up_third, w_out, last_rows)
    d_proj = attend_backward(p_near, p_far, d_near, d_mid, d_last)
    pair_d, pair_u_near, pair_u_mid, pair_u_last = (
        move(values, CORE)
        for values in after(
            (d_proj, u_near, u_mid, u_last), d_proj, pair_n_near, pair_n_far, pair_attended
        )
    )

    def exchange(value, step):
        return value + move(value, BUTTERFLY[step])

    *rows, gain_sum = input_terms(after(d_proj, pair_n_near, pair_n_far, pair_attended), w_qkv, n_near, n_far, ln_gain)
    own, behind, ahead, across, back, forth, top, bottom, gain_sum = after(
        (*rows, gain_sum.reshape(48, 128)), pair_d, pair_u_near, pair_u_mid, pair_u_last
    )
    gain_sum = exchange(gain_sum, 0)
    by_back, by_forth = move(top, X_BWD), move(bottom, X_FWD)

    operands = (n_near, n_far, pair_n_near, pair_n_far, u_near, u_mid, u_last)
    operands += (pair_u_near, pair_u_mid, pair_u_last)
    operands += (d_proj, pair_d, attended, pair_attended)
    far = weight_terms(blocks, 0, 1, after(operands, gain_sum))
    gain_sum = exchange(gain_sum, 1)
    g_top, g_bottom = after(far, gain_sum)
    g_by_back, g_by_forth = move(g_top, Y_BWD), move(g_bottom, Y_FWD)
    gain_sum = exchange(after(gain_sum, g_top, g_bottom), 2)
    g_back, g_forth, g_across = weight_terms(blocks, 1, 3, after(operands, g_top, g_bottom))

    g_by_back, g_by_forth, gain_sum = after((g_by_back, g_by_forth, gain_sum), g_across)
    back, forth, by_back, by_forth, gain_sum = after(
        (back, forth, by_back, by_forth, gain_sum), g_by_back, g_by_forth
    )
    gain_sum = exchange(gain_sum, 3)
    back, forth = add_at((back, 1, by_back), (forth, 2, by_forth))
    by_back, by_forth = move(back, X_BWD), move(forth, X_FWD)
    g_by_back, g_by_forth = after((g_by_back, g_by_forth), back, forth)
    g_back, g_forth = add_at((g_back, 1, g_by_back), (g_forth, 1, g_by_forth))
    g_by_across = move(after(g_across, g_back, g_forth), Z_HIGH)
    g_back, g_forth = after((g_back, g_forth), gain_sum)
    g_by_back, g_by_forth = move(g_back, Y_BWD), move(g_forth, Y_FWD)
    (near,) = weight_terms(blocks, 4, 4, after(operands, g_back, g_forth))

    by_back, by_forth = after((by_back, by_forth), near)
    gain_sum = exchange(after(gain_sum, by_back, by_forth), 4)
    across = (across.astype(F32) + by_back[1:].astype(F32) + by_forth[1:].astype(F32)).astype(BF)
    behind = behind.at[0].set(add(behind[0], by_back[0]))
    ahead = ahead.at[1].set(add(ahead[1], by_forth[0]))
    across = after(across, gain_sum)
    by_across = move(across, Z_LOW)
    by_behind = move(after(behind, across), X_BWD)

    g_by_back, g_by_forth, g_by_across = after((g_by_back, g_by_forth, g_by_across), behind, ahead)
    g_behind = add(near[0], halves(g_by_back[0], g_by_across[0]))
    g_ahead = add(near[1], halves(g_by_across[1], g_by_forth[0]))
    g_over = add(near[2], halves(g_by_back[1], g_by_forth[1]))
    g_terms = (near, move(g_behind, Y_BWD), move(g_ahead, Y_FWD), move(g_over, Z_HIGH))

    gain_sum = exchange(after(gain_sum, by_behind, by_across, g_over), 5)
    by_ahead = move(after(ahead, by_behind, by_across), X_FWD)
    gain_sum = exchange(after(gain_sum, ahead), 6)
    grad_gain = gain_sum.reshape(D)

    terms = (own, by_behind, by_ahead, by_across)
    d_normed = sum(t.astype(F32) for t in terms).reshape(64, D)
    normal, inverse = layer_stats(inputs.astype(F32))
    grad_inputs = (
        upstream.astype(F32) + norm_back(d_normed * ln_gain, normal, inverse)
    ).astype(BF)

    grad_qkv, grad_out = weight_sums(g_terms)
    return (grad_inputs, grad_qkv, grad_out, grad_gain)


def solution(mesh):
    placed = (
        P(("dp", "tensor"), None),
        P(("dp", "tensor"), None),
        P(None, None, "tensor"),
        P("tensor", None),
        P(),
    )
    return jax.shard_map(
        body,
        mesh=mesh,
        in_specs=placed,
        out_specs=(P(("dp", "tensor"), None), P(None, "dp", "tensor"), P("tensor", "dp"), P()),
        check_vma=False,
    )
```

```python
import math

import jax
import jax.numpy as jnp
from jax import lax
from jax.experimental import pallas as pl
from jax.experimental.pallas import tpu as pltpu
from jax.sharding import PartitionSpec as P

HD = 128
EPSILON = 1e-06
D = 6144
W = 384
BF = jnp.bfloat16
F32 = jnp.float32
MIB = 1 << 20
LIMIT_IT = 51
LIMIT_WT = 51
LIMIT_PR = 51
SHARE = 20

X_FWD = ("tensor", [(z * 4 + x, z * 4 + (x + 1) % 4) for z in range(2) for x in range(4)])
X_BWD = ("tensor", [(z * 4 + x, z * 4 + (x + 3) % 4) for z in range(2) for x in range(4)])
Z_LOW = ("tensor", [(z * 4 + x, (1 - z) * 4 + x) for z in range(2) for x in range(4)])
Y_FWD = ("dp", [(y * 4 + r, (y + 1) % 4 * 4 + r) for y in range(4) for r in range(4)])
Y_BWD = ("dp", [(y * 4 + r, (y + 3) % 4 * 4 + r) for y in range(4) for r in range(4)])
Z_HIGH = ("dp", [(i, i ^ 2) for i in range(16)])
CORE = ("dp", [(i, i ^ 1) for i in range(16)])
BUTTERFLY = [
    CORE,
    Z_HIGH,
    ("dp", [(i, i ^ 4) for i in range(16)]),
    ("dp", [(i, i ^ 8) for i in range(16)]),
    Z_LOW,
    ("tensor", [(i, i ^ 1) for i in range(8)]),
    ("tensor", [(i, i ^ 2) for i in range(8)]),
]


def move(value, route):
    return lax.ppermute(value, route[0], route[1])


def params(limit):
    return pltpu.CompilerParams(vmem_limit_bytes=limit * MIB)


def cost(flops, nbytes):
    return pl.CostEstimate(flops=int(flops) // SHARE, bytes_accessed=int(nbytes) // SHARE, transcendentals=0)


def layer_stats(values):
    average = jnp.mean(values, axis=-1, keepdims=True)
    centered = values - average
    inverse = lax.rsqrt(jnp.mean(centered * centered, axis=-1, keepdims=True) + EPSILON)
    return (centered * inverse, inverse)


def norm_back(grad, normal, inverse):
    return inverse * (
        grad
        - jnp.mean(grad, axis=-1, keepdims=True)
        - normal * jnp.mean(grad * normal, axis=-1, keepdims=True)
    )


def after(value, *others):
    return lax.optimization_barrier((value, others))[0]


def gather_stacks(near):
    _, behind, ahead, across = near
    return (
        jnp.stack([behind[0], across[0]]),
        jnp.stack([ahead[1], across[1]]),
        jnp.stack([behind[1], ahead[0]]),
    )


def gather_first(own, *before_swap):
    return (own, move(own, X_FWD), move(own, X_BWD), move(after(own, *before_swap), Z_LOW))


def gather_second(stacks):
    return tuple(move(s, route) for s, route in zip(stacks, (X_FWD, X_BWD, Z_LOW)))


def gather_third(pieces):
    return (move(pieces[0], X_FWD), move(pieces[1], X_BWD))


def near_rows(refs):
    return [r[i] for r in refs for i in range(2)]


def middle_rows(refs):
    fb, fa, fz = refs
    return [fb[0], fa[0], fb[1], fz[0], fz[1], fa[1]]


def last_rows(refs):
    return [r[...] for r in refs]


def far_rows(refs):
    return middle_rows(refs[:3]) + last_rows(refs[3:])


def add(a, b):
    return (a.astype(F32) + b.astype(F32)).astype(BF)


def halves(top, bottom):
    return jnp.stack([top, bottom])


def add_at(*sums):
    def kernel(*refs):
        count = len(sums)
        for values, term, out in zip(refs[:count], refs[count : 2 * count], refs[2 * count :]):
            out[0] = add(values[0], term[...])

    def placed(values, index):
        zeros = (0,) * (values.ndim - 1)
        return pl.BlockSpec((1,) + values.shape[1:], lambda i: (index,) + zeros)

    def whole(term):
        return pl.BlockSpec(term.shape, lambda i: (0,) * term.ndim)

    spots = [placed(values, index) for values, index, _ in sums]
    return pl.pallas_call(
        kernel,
        grid=(1,),
        in_specs=spots + [whole(term) for _, _, term in sums],
        out_specs=spots,
        out_shape=[jax.ShapeDtypeStruct(values.shape, BF) for values, _, _ in sums],
        input_output_aliases={i: i for i in range(len(sums))},
        compiler_params=params(LIMIT_PR),
        cost_estimate=cost(0, sum(term.size * 6 for _, _, term in sums)),
        name="add_at",
    )(*(values for values, _, _ in sums), *(term for _, _, term in sums))


def norm_rows(pieces, gain, picker):
    size = sum(piece.size for piece in pieces) // D

    def kernel(*refs):
        gain_ref, out_ref = refs[-2:]
        for at, rows in enumerate(picker(refs[:-2])):
            normal, _ = layer_stats(rows.astype(F32))
            out_ref[32 * at : 32 * at + 32, :] = (normal * gain_ref[...]).astype(BF)

    return pl.pallas_call(
        kernel,
        out_shape=jax.ShapeDtypeStruct((size, D), BF),
        compiler_params=params(20),
        cost_estimate=cost(size * D * 10, size * D * 4),
        name="norm_rows",
    )(*pieces, gain.reshape(1, D))


def wide(ref):
    return jnp.concatenate([ref[0], ref[1], ref[2]], axis=1)


def project_rows(normed, weight):
    step = 1536
    size = normed.shape[0]

    def kernel(x_ref, w_ref, out_ref):
        @pl.when(pl.program_id(0) == 0)
        def _():
            out_ref[...] = jnp.zeros_like(out_ref)

        out_ref[...] += jnp.dot(x_ref[...], wide(w_ref), preferred_element_type=F32)

    return pl.pallas_call(
        kernel,
        grid=(D // step,),
        in_specs=[
            pl.BlockSpec((size, step), lambda k: (0, k)),
            pl.BlockSpec((3, step, W), lambda k: (0, k, 0)),
        ],
        out_specs=pl.BlockSpec((size, 3 * W), lambda k: (0, 0)),
        out_shape=jax.ShapeDtypeStruct((size, 3 * W), F32),
        compiler_params=params(LIMIT_PR),
        cost_estimate=cost(2 * size * D * 3 * W, 3 * D * W * 2 + size * D * 2),
        name="project_rows",
    )(normed, weight)


def upstream_rows(pieces, w_out, picker):
    step = 1536
    size = sum(piece.size for piece in pieces) // D

    def kernel(*refs):
        w_ref, cat_ref, out_ref, acc = refs[-4:]
        k = pl.program_id(0)

        @pl.when(k == 0)
        def _():
            acc[...] = jnp.zeros_like(acc)

        for at, rows in enumerate(picker(refs[:-4])):
            cat_ref[32 * at : 32 * at + 32, :] = rows
        acc[...] += dot_nt(cat_ref[...], w_ref[...])

        @pl.when(k == D // step - 1)
        def _():
            out_ref[...] = acc[...].astype(BF)

    specs = [
        pl.BlockSpec((2, 32, step), lambda k: (0, 0, k))
        if piece.ndim == 3
        else pl.BlockSpec((32, step), lambda k: (0, k))
        for piece in pieces
    ]
    return pl.pallas_call(
        kernel,
        grid=(D // step,),
        in_specs=specs + [pl.BlockSpec((W, step), lambda k: (0, k))],
        out_specs=[
            pl.BlockSpec((size, step), lambda k: (0, k)),
            pl.BlockSpec((size, W), lambda k: (0, 0)),
        ],
        out_shape=[jax.ShapeDtypeStruct((size, D), BF), jax.ShapeDtypeStruct((size, W), BF)],
        scratch_shapes=[pltpu.VMEM((size, W), F32)],
        compiler_params=params(LIMIT_PR),
        cost_estimate=cost(2 * size * D * W, D * W * 2 + size * D * 4),
        name="upstream_rows",
    )(*pieces, w_out)


SCALE = 1.0 / math.sqrt(HD)


def dot_nt(a, b):
    return lax.dot_general(a, b, (((1,), (1,)), ((), ())), preferred_element_type=F32)


def dot_tn(a, b):
    return lax.dot_general(a, b, (((0,), (0,)), ((), ())), preferred_element_type=F32)


def dot_nn(a, b):
    return jnp.dot(a, b, preferred_element_type=F32)


def join(refs):
    return jnp.concatenate([r[...] for r in refs], axis=0)


def head_specs():
    return [
        pl.BlockSpec((256, HD), lambda h, s=s: (0, s * (W // HD) + h)) for s in range(3) for _ in range(2)
    ]


def attend_forward(near, far):
    def kernel(q1, q2, k1, k2, v1, v2, out_ref):
        query, _ = layer_stats(join((q1, q2)))
        key, _ = layer_stats(join((k1, k2)))
        value = join((v1, v2)).astype(BF)
        exponent = jnp.exp(dot_nt(query.astype(BF), key.astype(BF)) * SCALE)
        attention = exponent / jnp.sum(exponent, axis=-1, keepdims=True)
        out_ref[...] = dot_nn(attention.astype(BF), value).astype(BF)

    return pl.pallas_call(
        kernel,
        grid=(W // HD,),
        in_specs=head_specs(),
        out_specs=pl.BlockSpec((512, HD), lambda h: (0, h)),
        out_shape=jax.ShapeDtypeStruct((512, W), BF),
        compiler_params=params(40),
        cost_estimate=cost(3 * 4 * 512 * 512 * HD, 3 * 512 * W * 4),
        name="attend_forward",
    )(*(near, far) * 3)


def attend_backward(near, far, *d_pieces):
    def kernel(q1, q2, k1, k2, v1, v2, d1, d2, d3, out_ref):
        def put(s, values):
            column = pl.multiple_of(s * W + pl.program_id(0) * HD, HD)
            out_ref[:, pl.ds(column, HD)] = values.astype(BF)

        query, query_inv = layer_stats(join((q1, q2)))
        key, key_inv = layer_stats(join((k1, k2)))
        value_low = join((v1, v2)).astype(BF)
        query_low = query.astype(BF)
        key_low = key.astype(BF)
        d_att = join((d1, d2, d3))
        exponent = jnp.exp(dot_nt(query_low, key_low) * SCALE)
        attention = exponent / jnp.sum(exponent, axis=-1, keepdims=True)
        d_raw = dot_nt(d_att, value_low)
        put(2, dot_tn(attention.astype(BF), d_att))
        inner = jnp.sum(d_raw * attention, axis=-1, keepdims=True)
        d_scores = (attention * (d_raw - inner) * SCALE).astype(BF)
        put(0, norm_back(dot_nn(d_scores, key_low), query, query_inv))
        put(1, norm_back(dot_tn(d_scores, query_low), key, key_inv))

    return pl.pallas_call(
        kernel,
        grid=(W // HD,),
        in_specs=head_specs() + [pl.BlockSpec((d.shape[0], HD), lambda h: (0, h)) for d in d_pieces],
        out_specs=pl.BlockSpec((512, 3 * W), lambda h: (0, 0)),
        out_shape=jax.ShapeDtypeStruct((512, 3 * W), BF),
        compiler_params=params(48),
        cost_estimate=cost(3 * 10 * 512 * 512 * HD, 3 * 512 * W * 8),
        name="attend_backward",
    )(*(near, far) * 3, *d_pieces)


def input_terms(d_proj, weight, n_near, n_far, gain):
    step = 1024
    far = {(4, 0): (4, 0), (5, 0): (4, 1), (5, 1): (4, 2), (4, 1): (5, 0), (6, 0): (5, 1), (6, 1): (5, 2)}

    def kernel(d_ref, w_ref, n1, n2, gain_ref, *outs):
        term = dot_nt(d_ref[...], wide(w_ref))
        for at in range(8):
            for half in range(2):
                low = 64 * at + 32 * half
                rows = term[low : low + 32].astype(BF)
                if at < 4:
                    outs[at][half] = rows
                elif at < 7:
                    out, row = far[at, half]
                    outs[out][row] = rows
                else:
                    outs[6 + half][...] = rows
        sums = jnp.sum(term * join((n1, n2)).astype(F32), axis=0, keepdims=True)
        outs[8][...] = sums / gain_ref[...]

    return pl.pallas_call(
        kernel,
        grid=(D // step,),
        in_specs=[
            pl.BlockSpec((512, 3 * W), lambda k: (0, 0)),
            pl.BlockSpec((3, step, W), lambda k: (0, k, 0)),
            pl.BlockSpec((256, step), lambda k: (0, k)),
            pl.BlockSpec((256, step), lambda k: (0, k)),
            pl.BlockSpec((1, step), lambda k: (0, k)),
        ],
        out_specs=[pl.BlockSpec((2, 32, step), lambda k: (0, 0, k))] * 4
        + [pl.BlockSpec((3, 32, step), lambda k: (0, 0, k))] * 2
        + [pl.BlockSpec((32, step), lambda k: (0, k))] * 2
        + [pl.BlockSpec((1, step), lambda k: (0, k))],
        out_shape=[jax.ShapeDtypeStruct((2, 32, D), BF)] * 4
        + [jax.ShapeDtypeStruct((3, 32, D), BF)] * 2
        + [jax.ShapeDtypeStruct((32, D), BF)] * 2
        + [jax.ShapeDtypeStruct((1, D), F32)],
        compiler_params=params(LIMIT_IT),
        cost_estimate=cost(2 * 512 * D * 3 * W, 3 * D * W * 2 + 512 * D * 4),
        name="input_terms",
    )(d_proj, weight, n_near, n_far, gain.reshape(1, D))


def weight_terms(blocks, first, count, operands):
    def kernel(_, n1, n2, m1, m2, u1, u2, u3, v1, v2, v3, d_ref, e_ref, a_ref, b_ref, *outs):
        total = dot_tn(join((n1, n2)), d_ref[...]) + dot_tn(join((m1, m2)), e_ref[...])
        total = total.astype(BF)
        other = dot_tn(a_ref[...], join((u1, u2, u3))) + dot_tn(b_ref[...], join((v1, v2, v3)))
        other = other.astype(BF)

        def put(half, place):
            low = 192 * half
            for s in range(3):
                place(s, total[low : low + 192, s * W : (s + 1) * W])
            place(3, other[low : low + 192])

        def put_in(half, ref, index):
            def place(s, values):
                ref[index + (s,)] = values

            put(half, place)

        if count == 1:
            put_in(0, outs[0], ())
            put_in(1, outs[1], ())
        elif count == 4:
            put_in(0, outs[0], (0, 0))
            put_in(1, outs[0], (0, 1))
        else:
            back, forth, across = outs
            for k, (top, bottom) in enumerate(
                [((back, 0), (forth, 0)), ((back, 1), (across, 0)), ((across, 1), (forth, 1))]
            ):

                @pl.when(pl.program_id(0) == k)
                def _():
                    put_in(0, top[0], (top[1],))
                    put_in(1, bottom[0], (bottom[1],))

    placed = [
        pl.BlockSpec((rows.shape[0], W), lambda k, b: (0, b[first + k])) for rows in operands[:10]
    ]
    flat = pl.BlockSpec((512, 3 * W), lambda k, b: (0, 0))
    narrow = pl.BlockSpec((512, W), lambda k, b: (0, 0))
    if count == 1:
        shapes = [(4, 192, W)] * 2
    elif count == 3:
        shapes = [(2, 4, 192, W)] * 3
    else:
        shapes = [(count, 2, 4, 192, W)]
    if count == 4:
        specs = [pl.BlockSpec((1, 2, 4, 192, W), lambda k, b: (k, 0, 0, 0, 0))]
    else:
        specs = [pl.BlockSpec(shape, lambda k, b, n=len(shape): (0,) * n) for shape in shapes]
    return pl.pallas_call(
        kernel,
        grid_spec=pltpu.PrefetchScalarGridSpec(
            num_scalar_prefetch=1,
            grid=(count,),
            in_specs=placed + [flat, flat, narrow, narrow],
            out_specs=specs,
        ),
        out_shape=[jax.ShapeDtypeStruct(shape, BF) for shape in shapes],
        compiler_params=params(LIMIT_WT),
        cost_estimate=cost(count * 8 * W * W * 1024, count * 4 * W * W * 2 + 4 * 1024 * W * 2),
        name="weight_terms",
    )(blocks, *operands)


def weight_sums(terms):
    def kernel(own, *refs):
        qkv_ref, out_ref = refs[-2:]
        for half in range(2):
            for s in range(4):
                total = own[0, half, s].astype(F32)
                for ref in refs[:3]:
                    total += ref[half, s].astype(F32)
                if s < 3:
                    qkv_ref[s, 192 * half : 192 * half + 192, :] = total
                else:
                    out_ref[192 * half : 192 * half + 192, :] = total

    near, *others = terms
    whole = pl.BlockSpec((2, 4, 192, W), lambda i: (0, 0, 0, 0))
    return pl.pallas_call(
        kernel,
        grid=(1,),
        in_specs=[pl.BlockSpec((1, 2, 4, 192, W), lambda i: (3, 0, 0, 0, 0))] + [whole] * 3,
        out_specs=[
            pl.BlockSpec((3, W, W), lambda i: (0, 0, 0)),
            pl.BlockSpec((W, W), lambda i: (0, 0)),
        ],
        out_shape=[jax.ShapeDtypeStruct((3, W, W), F32), jax.ShapeDtypeStruct((W, W), F32)],
        compiler_params=params(24),
        cost_estimate=cost(16 * W * W, 4 * 4 * W * W * 3),
        name="weight_sums",
    )(near, *others)


def body(inputs, upstream, w_qkv, w_out, ln_gain):
    place = lax.axis_index("dp")
    y, zh, core = place // 4, (place // 2) % 2, place % 2
    offsets = [(2, 1), (2, 0), (3, 1), (1, 1), (3, 0), (1, 0), (0, 1), (0, 0)]
    blocks = jnp.stack([(y + dy) % 4 * 4 + (zh ^ dz) * 2 + core for dy, dz in offsets])
    blocks = blocks.astype(jnp.int32)

    in_near = gather_first(inputs.reshape(2, 32, D))
    in_stacks = gather_stacks(in_near)
    in_second = gather_second(in_stacks)
    up_near = gather_first(after(upstream.reshape(2, 32, D), in_stacks), in_second)

    n_near = norm_rows(in_near, ln_gain, near_rows)
    p_near = project_rows(n_near, w_qkv)

    in_second = after(in_second, p_near)
    in_third = gather_third((in_second[0][1], in_second[1][1]))
    n_mid = norm_rows(in_second, ln_gain, middle_rows)
    p_mid = project_rows(n_mid, w_qkv)
    in_third = after(in_third, p_mid)
    up_stacks = gather_stacks(after(up_near, in_third))
    up_second = gather_second(up_stacks)

    n_last = norm_rows(after(in_third, up_stacks), ln_gain, last_rows)
    p_last = project_rows(n_last, w_qkv)
    n_far = jnp.concatenate([n_mid, n_last])
    p_far = jnp.concatenate([p_mid, p_last])
    u_near, d_near = upstream_rows(after(up_near, p_far), w_out, near_rows)
    attended = attend_forward(p_near, after(p_far, d_near))

    up_second = after(up_second, attended)
    up_pieces = (up_second[0][1], up_second[1][1])
    up_third = gather_third(up_pieces)
    u_mid, d_mid = upstream_rows(after(up_second, up_pieces), w_out, middle_rows)
    up_third = after(up_third, d_mid)

    pair_n_near, pair_n_far, pair_attended = (
        move(values, CORE) for values in after((n_near, n_far, attended), up_third)
    )
    u_last, d_last = upstream_rows(up_third, w_out, last_rows)
    d_proj = attend_backward(p_near, p_far, d_near, d_mid, d_last)
    pair_d, pair_u_near, pair_u_mid, pair_u_last = (
        move(values, CORE)
        for values in after(
            (d_proj, u_near, u_mid, u_last), d_proj, pair_n_near, pair_n_far, pair_attended
        )
    )

    def exchange(value, step):
        return value + move(value, BUTTERFLY[step])

    *rows, gain_sum = input_terms(after(d_proj, pair_n_near, pair_n_far, pair_attended), w_qkv, n_near, n_far, ln_gain)
    own, behind, ahead, across, back, forth, top, bottom, gain_sum = after(
        (*rows, gain_sum.reshape(48, 128)), pair_d, pair_u_near, pair_u_mid, pair_u_last
    )
    gain_sum = exchange(gain_sum, 0)
    by_back, by_forth = move(top, X_BWD), move(bottom, X_FWD)

    operands = (n_near, n_far, pair_n_near, pair_n_far, u_near, u_mid, u_last)
    operands += (pair_u_near, pair_u_mid, pair_u_last)
    operands += (d_proj, pair_d, attended, pair_attended)
    far = weight_terms(blocks, 0, 1, after(operands, gain_sum))
    gain_sum = exchange(gain_sum, 1)
    g_top, g_bottom = after(far, gain_sum)
    g_by_back, g_by_forth = move(g_top, Y_BWD), move(g_bottom, Y_FWD)
    gain_sum = exchange(after(gain_sum, g_top, g_bottom), 2)
    g_back, g_forth, g_across = weight_terms(blocks, 1, 3, after(operands, g_top, g_bottom))

    g_by_back, g_by_forth, gain_sum = after((g_by_back, g_by_forth, gain_sum), g_across)
    back, forth, by_back, by_forth, gain_sum = after(
        (back, forth, by_back, by_forth, gain_sum), g_by_back, g_by_forth
    )
    gain_sum = exchange(gain_sum, 3)
    back, forth = add_at((back, 1, by_back), (forth, 2, by_forth))
    by_back, by_forth = move(back, X_BWD), move(forth, X_FWD)
    g_by_back, g_by_forth = after((g_by_back, g_by_forth), back, forth)
    g_back, g_forth = add_at((g_back, 1, g_by_back), (g_forth, 1, g_by_forth))
    g_by_across = move(after(g_across, g_back, g_forth), Z_HIGH)
    g_back, g_forth = after((g_back, g_forth), gain_sum)
    g_by_back, g_by_forth = move(g_back, Y_BWD), move(g_forth, Y_FWD)
    (near,) = weight_terms(blocks, 4, 4, after(operands, g_back, g_forth))

    by_back, by_forth = after((by_back, by_forth), near)
    gain_sum = exchange(after(gain_sum, by_back, by_forth), 4)
    across = (across.astype(F32) + by_back[1:].astype(F32) + by_forth[1:].astype(F32)).astype(BF)
    behind = behind.at[0].set(add(behind[0], by_back[0]))
    ahead = ahead.at[1].set(add(ahead[1], by_forth[0]))
    across = after(across, gain_sum)
    by_across = move(across, Z_LOW)
    by_behind = move(after(behind, across), X_BWD)

    g_by_back, g_by_forth, g_by_across = after((g_by_back, g_by_forth, g_by_across), behind, ahead)
    g_behind = add(near[0], halves(g_by_back[0], g_by_across[0]))
    g_ahead = add(near[1], halves(g_by_across[1], g_by_forth[0]))
    g_over = add(near[2], halves(g_by_back[1], g_by_forth[1]))
    g_terms = (near, move(g_behind, Y_BWD), move(g_ahead, Y_FWD), move(g_over, Z_HIGH))

    gain_sum = exchange(after(gain_sum, by_behind, by_across, g_over), 5)
    by_ahead = move(after(ahead, by_behind, by_across), X_FWD)
    gain_sum = exchange(after(gain_sum, ahead), 6)
    grad_gain = gain_sum.reshape(D)

    terms = (own, by_behind, by_ahead, by_across)
    d_normed = sum(t.astype(F32) for t in terms).reshape(64, D)
    normal, inverse = layer_stats(inputs.astype(F32))
    grad_inputs = (
        upstream.astype(F32) + norm_back(d_normed * ln_gain, normal, inverse)
    ).astype(BF)

    grad_qkv, grad_out = weight_sums(g_terms)
    return (grad_inputs, grad_qkv, grad_out, grad_gain)


def solution(mesh):
    placed = (
        P(("dp", "tensor"), None),
        P(("dp", "tensor"), None),
        P(None, None, "tensor"),
        P("tensor", None),
        P(),
    )
    return jax.shard_map(
        body,
        mesh=mesh,
        in_specs=placed,
        out_specs=(P(("dp", "tensor"), None), P(None, "dp", "tensor"), P("tensor", "dp"), P()),
        check_vma=False,
    )
```
